32 devices in a mesh: scene: 2 (over x), view: 16 (over z, y, core).
Axes of the slice: x: 2, y: 2, z: 4, core: 2. Of those that a mesh axis runs over, the one named last changes fastest.
Arguments:
- latents: bfloat16 [64, 256, 1024], P(('scene', 'view')), parts along dimension 0, may hold values from -6 to 6
- mod_scale: float32 [64, 1024], P(('scene', 'view')), parts along dimension 0
- observed: bfloat16 [2048, 1024], P(('scene', 'view')), parts along dimension 0, may hold values from -6 to 6
- w_query: bfloat16 [1024, 1024], replicated, may hold values from -0.1875 to 0.1875
- w_keyval: bfloat16 [1024, 2048], replicated, may hold values from -0.1875 to 0.1875
- w_out: bfloat16 [1024, 1024], replicated, may hold values from -3 to 3
- pair_views: int32 [64, 5], P(('scene', 'view')), parts along dimension 0, may hold values from 0 to 31, as said below
- pair_count: int32 [64], P(('scene', 'view')), parts along dimension 0, may hold values from 1 to 5
- cond_views: int32 [64, 4], P(('scene', 'view')), parts along dimension 0, may hold values from 0 to 3, as said below
- cond_count: int32 [64], P(('scene', 'view')), parts along dimension 0, may hold values from 1 to 4
- obs_count: int32 [8], P('scene'), parts along dimension 0, may hold values from 128 to 256
Outputs:
- attended: bfloat16 [64, 256, 1024], P(('scene', 'view')), parts along dimension 0
The draws below stay inside these ranges and needn't reach their ends.
There are 2 independent parts, one for each index of `scene`. The reference program is written for one: setup_inputs(seed, part) draws one part's arguments, and reference() takes and returns one part's arrays. A program takes and returns all parts, laid end to end along the dimension named above; an argument that names none is the same for every part. Nothing has to cross between parts.
Inputs may be any that keep to these rules, and one draw needn't show every extreme that they name: `pair_views`: slot 0 is the view itself; the slots below pair_count[v] are distinct views at most 2 places from v around the cycle of 32 views; later slots repeat v. `cond_views`: the slots below cond_count[v] are distinct observed views; later slots repeat slot 0.
All inputs are finite; a program needn't handle non-finite values.
Results may differ from the reference program's by a relative error of at most 0.004.
The reference program's roundings to bfloat16 on the way (of `modulated`, `obs_keyval`, `probs` and `heads_out`) count: a program that leaves them out, or rounds other values in their place, can miss the bound.
Values may be sent and summed in bfloat16 or wider, within the bound.
A program may use at most 128 MiB of HBM per device.

```python
import jax
import jax.numpy as jnp
from jax import lax

D = 1024
HEADS = 16
HD = 64
TOKV = 256
REACH = 2
PMAX = 5
VIEWS = 32
OBS = 4
OBS_ROWS = 1024


def intersection_lists(key):
    order_keys = jax.random.split(jax.random.fold_in(key, 11), VIEWS)
    offsets = jax.vmap(lambda sub: jax.random.permutation(sub, 2 * REACH))(order_keys)
    signed = jnp.where(offsets < REACH, offsets - REACH, offsets - REACH + 1)
    count = jax.random.randint(jax.random.fold_in(key, 12), (VIEWS,), 1, PMAX + 1)
    count = count.at[0].set(PMAX).at[1].set(1)
    view_ids = jnp.arange(VIEWS)
    listed = jnp.concatenate([view_ids[:, None], (view_ids[:, None] + signed) % VIEWS], axis=1)
    slot_ids = jnp.arange(PMAX)
    lists = jnp.where(slot_ids[None, :] < count[:, None], listed, view_ids[:, None])
    return (lists.astype(jnp.int32), count.astype(jnp.int32))


def conditioning_lists(key):
    order_keys = jax.random.split(jax.random.fold_in(key, 21), VIEWS)
    order = jax.vmap(lambda sub: jax.random.permutation(sub, OBS))(order_keys)
    count = jax.random.randint(jax.random.fold_in(key, 22), (VIEWS,), 1, OBS + 1)
    count = count.at[0].set(OBS).at[1].set(1)
    slot_ids = jnp.arange(OBS)
    lists = jnp.where(slot_ids[None, :] < count[:, None], order, order[:, :1])
    return (lists.astype(jnp.int32), count.astype(jnp.int32))


def draw_pair_views(key, part):
    return intersection_lists(key)[0]


def draw_pair_count(key, part):
    return intersection_lists(key)[1]


def draw_cond_views(key, part):
    return conditioning_lists(key)[0]


def draw_cond_count(key, part):
    return conditioning_lists(key)[1]


def draw_obs_count(key, part):
    key = jax.random.fold_in(key, 31)
    count = jax.random.randint(key, (OBS,), TOKV // 2, TOKV + 1)
    return count.at[0].set(TOKV).at[1].set(TOKV // 2).astype(jnp.int32)


def draw_mod_scale(key, part):
    key = jax.random.fold_in(key, 41)
    noise = jnp.clip(jax.random.normal(jax.random.fold_in(key, 1), (VIEWS, D), jnp.float32), -3.0, 3.0)
    return (1.0 + 0.3 * noise).astype(jnp.float32)


def steps_of(key, extent, cuts, smallest, largest):
    loudness, own = 1.0, jax.random.fold_in(key, 6)
    for position, blocks in cuts:
        heights = jnp.exp(jax.random.uniform(jax.random.fold_in(own, position), (blocks,), jnp.float32, smallest / len(cuts), largest / len(cuts)))
        loudness = loudness * jnp.repeat(heights, extent[position] // blocks).reshape([-1 if axis == position else 1 for axis in range(len(extent))])
    return loudness


def scatter_about(rng, extent, width, limit, shards=(), kind=jnp.bfloat16):
    drawn = jax.random.normal(rng, extent, jnp.float32) * width
    if len(shards) > 0:
        drawn = steps_of(rng, extent, shards, -0.22, 0.18) * drawn
    return jnp.clip(drawn, min=-limit, max=limit).astype(kind)


def setup_inputs(seed: int = 0, part: int = 0) -> dict:
    splits = jax.random.split(jax.random.key(seed), 12)
    own_keys = jax.random.split(jax.random.fold_in(splits[11], part), 12)
    latents = scatter_about(own_keys[0], (VIEWS, TOKV, D), 1.0, 6.0, ((0, 16),))
    mod_scale = draw_mod_scale(jax.random.fold_in(jax.random.fold_in(splits[11], part), 71), part)
    observed = scatter_about(own_keys[2], (OBS_ROWS, D), 1.0, 6.0, ((0, 16),))
    w_query = scatter_about(splits[3], (D, D), D ** -0.5, 0.1875)
    w_keyval = scatter_about(splits[4], (D, 2 * D), D ** -0.5, 0.1875)
    w_out = scatter_about(splits[5], (D, D), (max(D // 256, 1)) ** -0.5, 3.0)
    pair_views = draw_pair_views(jax.random.fold_in(jax.random.fold_in(splits[11], part), 71), part)
    pair_count = draw_pair_count(jax.random.fold_in(jax.random.fold_in(splits[11], part), 71), part)
    cond_views = draw_cond_views(jax.random.fold_in(jax.random.fold_in(splits[11], part), 71), part)
    cond_count = draw_cond_count(jax.random.fold_in(jax.random.fold_in(splits[11], part), 71), part)
    obs_count = draw_obs_count(jax.random.fold_in(jax.random.fold_in(splits[11], part), 71), part)
    return {"latents": latents, "mod_scale": mod_scale, "observed": observed, "w_query": w_query, "w_keyval": w_keyval, "w_out": w_out, "pair_views": pair_views, "pair_count": pair_count, "cond_views": cond_views, "cond_count": cond_count, "obs_count": obs_count}


def normalize(rows):
    values = rows.astype(jnp.float32)
    centered = values - lax.optimization_barrier(jnp.mean(values, axis=-1, keepdims=True))
    return centered * lax.rsqrt(lax.optimization_barrier(jnp.mean(centered * centered, axis=-1, keepdims=True)) + 1e-06)

def attend(query, keyval, live):
    keys_count = keyval.shape[0]
    q_heads = query.astype(jnp.float32).reshape(TOKV, HEADS, HD)
    k_heads = keyval[:, :D].astype(jnp.float32).reshape(keys_count, HEADS, HD)
    v_heads = keyval[:, D:].astype(jnp.float32).reshape(keys_count, HEADS, HD)
    scores = jnp.einsum('qhd,khd->hqk', q_heads, k_heads) * HD ** (-0.5)
    scores = jnp.where(live[None, None, :], scores, jnp.float32(-1e+30))
    top = lax.optimization_barrier(jnp.max(scores, axis=-1, keepdims=True))
    weights = jnp.exp(scores - top)
    probs = (weights / lax.optimization_barrier(jnp.sum(weights, axis=-1, keepdims=True))).astype(jnp.bfloat16)
    mixed = jnp.einsum('hqk,khd->qhd', probs.astype(jnp.float32), v_heads)
    return mixed.astype(jnp.bfloat16).reshape(TOKV, D)

def reference(latents, mod_scale, observed, w_query, w_keyval, w_out, pair_views, pair_count, cond_views, cond_count, obs_count):
    modulated = (normalize(latents) * mod_scale[:, None, :]).astype(jnp.bfloat16)
    flat = modulated.reshape(VIEWS * TOKV, D)
    query = jnp.dot(flat, w_query, preferred_element_type=jnp.float32).astype(jnp.bfloat16).reshape(VIEWS, TOKV, D)
    keyval = jnp.dot(flat, w_keyval, preferred_element_type=jnp.float32).astype(jnp.bfloat16).reshape(VIEWS, TOKV, 2 * D)
    obs_norm = normalize(observed).astype(jnp.bfloat16)
    obs_keyval = jnp.dot(obs_norm, w_keyval, preferred_element_type=jnp.float32).astype(jnp.bfloat16)
    view_ids = jnp.arange(VIEWS, dtype=jnp.int32)
    targets = (view_ids[:, None] + jnp.arange(PMAX, dtype=jnp.int32)[None, :] - REACH) % VIEWS
    pair_live = jnp.arange(PMAX, dtype=jnp.int32)[None, :] < pair_count[:, None]
    window_live = jnp.any((pair_views[:, None, :] == targets[:, :, None]) & pair_live[:, None, :], axis=-1)
    cond_live = jnp.arange(OBS, dtype=jnp.int32)[None, :] < cond_count[:, None]
    obs_ids = jnp.arange(OBS, dtype=jnp.int32)
    obs_live = jnp.any((cond_views[:, None, :] == obs_ids[None, :, None]) & cond_live[:, None, :], axis=-1)
    token_live = jnp.arange(TOKV, dtype=jnp.int32)[None, :] < obs_count[:, None]
    obs_key_live = (obs_live[:, :, None] & token_live[None, :, :]).reshape(VIEWS, OBS_ROWS)
    padded = jnp.concatenate([keyval[VIEWS - REACH:], keyval, keyval[:REACH]], axis=0)

    def one_view(index):
        window = lax.dynamic_slice_in_dim(padded, index, PMAX, 0).reshape(PMAX * TOKV, 2 * D)
        keys_all = jnp.concatenate([window, obs_keyval], axis=0)
        live = jnp.concatenate([jnp.repeat(window_live[index], TOKV), obs_key_live[index]])
        return attend(query[index], keys_all, live)
    heads_out = lax.map(one_view, view_ids)
    attended = jnp.dot(heads_out.reshape(VIEWS * TOKV, D), w_out, preferred_element_type=jnp.float32)
    return attended.astype(jnp.bfloat16).reshape(VIEWS, TOKV, D)
```

```python
import functools

import jax
import jax.numpy as jnp
from jax import lax
from jax.experimental import pallas as pl
from jax.experimental.pallas import tpu as pltpu
from jax.sharding import PartitionSpec as P

HEADS = 16
LANES = 128
DEAD = -1e30


def normalize(rows):
    values = rows.astype(jnp.float32)
    centered = values - jnp.mean(values, axis=-1, keepdims=True)
    return centered * lax.rsqrt(jnp.mean(centered * centered, axis=-1, keepdims=True) + 1e-06)


def dot_t(a, b):
    return lax.dot_general(a, b, (((1,), (1,)), ((), ())), preferred_element_type=jnp.float32)


def attention_kernel(view_dev, tok, size, slots, obs_views, *refs):
    (cap_ref, q_ref, kb_ref, vb_ref, ko_ref, vo_ref, ka_ref, va_ref, kx_ref, vx_ref, w_ref,
     out_ref, s0, s1, e0, e1, m0, m1, r0, r1, heads) = refs
    step = pl.program_id(0)
    halo = slots - 1
    blocks = slots + obs_views

    def key_block(view, j, key):
        before, own, after, obs = (
            (kb_ref, ko_ref, ka_ref, kx_ref) if key else (vb_ref, vo_ref, va_ref, vx_ref)
        )
        if j >= slots:
            return obs[pl.ds((j - slots) * tok, tok), :]
        place = view + j
        reach = halo // 2
        if place < reach:
            return before[pl.ds(place * tok, tok), :]
        if place < reach + view_dev:
            return own[pl.ds((place - reach) * tok, tok), :]
        return after[pl.ds((place - reach - view_dev) * tok, tok), :]

    lane = lax.broadcasted_iota(jnp.int32, (tok, LANES), 1)
    per_tile = LANES // size
    units = [(view, head) for view in range(view_dev) for head in range(per_tile)]
    score, expo, top, inv = (s0, s1), (e0, e1), (m0, m1), (r0, r1)
    total = [None] * len(units)
    mixed = [None] * view_dev
    tiles = tok // LANES
    for t in range(len(units) + 2):
        a, b, c = t, t - 1, t - 2
        if a < len(units):
            view, head = units[a]
            q_all = q_ref[pl.ds(view * tok, tok), :]
            mine = (lane >= head * size) & (lane < (head + 1) * size)
            q = jnp.where(mine, q_all.astype(jnp.float32) * size ** -0.5, 0.0).astype(jnp.bfloat16)
            high = None
        if 0 <= b < len(units):
            low = None
            m_b = top[b % 2][...]
        if 0 <= c < len(units):
            acc = None
            r_c = inv[c % 2][...]
        for j in range(blocks):
            if a < len(units):
                s = dot_t(q, key_block(view, j, True))
                s = jnp.minimum(s, cap_ref[view : view + 1, pl.ds(j * tok, tok)])
                score[a % 2][:, pl.ds(j * tok, tok)] = s
                for i in range(tiles):
                    part = s[:, i * LANES : (i + 1) * LANES]
                    high = part if high is None else jnp.maximum(high, part)
            if 0 <= b < len(units):
                for i in range(tiles):
                    cols = pl.ds(j * tok + i * LANES, LANES)
                    e = jnp.exp(score[b % 2][:, cols] - m_b)
                    expo[b % 2][:, cols] = e
                    low = e if low is None else low + e
            if 0 <= c < len(units):
                probs = jnp.concatenate(
                    [
                        (expo[c % 2][:, pl.ds(j * tok + i * LANES, LANES)] * r_c).astype(jnp.bfloat16)
                        for i in range(tiles)
                    ],
                    axis=1,
                )
                part = jnp.dot(
                    probs, key_block(units[c][0], j, False), preferred_element_type=jnp.float32
                )
                acc = part if acc is None else acc + part
        if a < len(units):
            top[a % 2][...] = jnp.broadcast_to(
                jnp.max(high, axis=1, keepdims=True), (tok, LANES)
            )
        if 0 <= b < len(units):
            inv[b % 2][...] = jnp.broadcast_to(
                1.0 / jnp.sum(low, axis=1, keepdims=True), (tok, LANES)
            )
        if 0 <= c < len(units):
            view_c, head_c = units[c]
            if head_c == 0:
                mixed[view_c] = acc
            else:
                mixed[view_c] = jnp.where(lane >= head_c * size, acc, mixed[view_c])
            if head_c == per_tile - 1:
                heads[pl.ds(view_c * tok, tok), pl.ds(pl.multiple_of(step * LANES, LANES), LANES)] = (
                    mixed[view_c].astype(jnp.bfloat16)
                )

    @pl.when(step == pl.num_programs(0) - 1)
    def _():
        for view in range(view_dev):
            rows = pl.ds(view * tok, tok)
            out_ref[rows, :] = jnp.dot(
                heads[rows, :], w_ref[...], preferred_element_type=jnp.float32
            ).astype(jnp.bfloat16)


def attention(cap, query, before, own, after, obs, w_out, view_dev, tok, size, slots, obs_views):
    rows, width = query.shape
    pairs = width // LANES
    keys = (slots + obs_views) * tok

    def halves(array):
        n = array.shape[0]
        return (
            pl.BlockSpec((n, LANES), lambda p: (0, p)),
            pl.BlockSpec((n, LANES), lambda p: (0, p + pairs)),
        )

    whole = lambda shape: pl.BlockSpec(shape, lambda p: (0, 0))
    return pl.pallas_call(
        functools.partial(attention_kernel, view_dev, tok, size, slots, obs_views),
        grid=(pairs,),
        in_specs=[
            whole(cap.shape),
            pl.BlockSpec((rows, LANES), lambda p: (0, p)),
            *halves(before),
            *halves(own),
            *halves(after),
            *halves(obs),
            whole(w_out.shape),
        ],
        out_specs=whole((rows, width)),
        out_shape=jax.ShapeDtypeStruct((rows, width), jnp.bfloat16),
        scratch_shapes=[
            pltpu.VMEM((tok, keys), jnp.float32),
            pltpu.VMEM((tok, keys), jnp.float32),
            pltpu.VMEM((tok, keys), jnp.float32),
            pltpu.VMEM((tok, keys), jnp.float32),
            pltpu.VMEM((tok, LANES), jnp.float32),
            pltpu.VMEM((tok, LANES), jnp.float32),
            pltpu.VMEM((tok, LANES), jnp.float32),
            pltpu.VMEM((tok, LANES), jnp.float32),
            pltpu.VMEM((rows, width), jnp.bfloat16),
        ],
        compiler_params=pltpu.CompilerParams(vmem_limit_bytes=40 * 1024 * 1024),
    )(cap, query, before, before, own, own, after, after, obs, obs, w_out)


def shards(
    latents,
    mod_scale,
    observed,
    w_query,
    w_keyval,
    w_out,
    pair_views,
    pair_count,
    cond_views,
    cond_count,
    obs_count,
):
    view_dev, tok, width = latents.shape
    slots = pair_views.shape[1]
    reach = (slots - 1) // 2
    peers = lax.axis_size("view")
    views = view_dev * peers
    first = lax.axis_index("view") * view_dev
    obs_views = obs_count.shape[0]
    obs_rows = lax.all_gather(observed, "view", axis=0, tiled=True)
    modulated = (normalize(latents) * mod_scale[:, None, :]).astype(jnp.bfloat16)
    flat = modulated.reshape(view_dev * tok, width)
    up = [(i, (i + 1) % peers) for i in range(peers)]
    down = [(j, i) for i, j in up]
    edge = reach * tok
    before = lax.ppermute(flat[flat.shape[0] - edge :], "view", up)
    after = lax.ppermute(flat[:edge], "view", down)

    def project(rows, weight):
        return jnp.dot(rows, weight, preferred_element_type=jnp.float32).astype(jnp.bfloat16)

    query = project(flat, w_query)
    own_kv = project(flat, w_keyval)
    obs_kv = project(normalize(obs_rows).astype(jnp.bfloat16), w_keyval)
    before_kv = project(before, w_keyval)
    after_kv = project(after, w_keyval)

    view_ids = first + jnp.arange(view_dev, dtype=jnp.int32)
    targets = (view_ids[:, None] + jnp.arange(slots, dtype=jnp.int32)[None, :] - reach) % views
    pair_live = jnp.arange(slots, dtype=jnp.int32)[None, :] < pair_count[:, None]
    window_live = jnp.any(
        (pair_views[:, None, :] == targets[:, :, None]) & pair_live[:, None, :], axis=-1
    )
    cond_live = jnp.arange(cond_views.shape[1], dtype=jnp.int32)[None, :] < cond_count[:, None]
    obs_ids = jnp.arange(obs_views, dtype=jnp.int32)
    obs_live = jnp.any(
        (cond_views[:, None, :] == obs_ids[None, :, None]) & cond_live[:, None, :], axis=-1
    )
    token_live = jnp.arange(tok, dtype=jnp.int32)[None, :] < obs_count[:, None]
    obs_key_live = (obs_live[:, :, None] & token_live[None, :, :]).reshape(
        view_dev, obs_views * tok
    )
    live = jnp.concatenate([jnp.repeat(window_live, tok, axis=1), obs_key_live], axis=1)
    cap = jnp.where(live, jnp.finfo(jnp.float32).max, jnp.float32(DEAD))
    out = attention(
        cap, query, before_kv, own_kv, after_kv, obs_kv, w_out,
        view_dev, tok, width // HEADS, slots, obs_views,
    )
    return out.reshape(view_dev, tok, width)


def solution(mesh):
    in_specs = (
        P(("scene", "view"), None, None),
        P(("scene", "view"), None),
        P(("scene", "view"), None),
        P(),
        P(),
        P(),
        P(("scene", "view"), None),
        P(("scene", "view")),
        P(("scene", "view"), None),
        P(("scene", "view")),
        P("scene"),
    )
    out_specs = P(("scene", "view"), None, None)
    return jax.shard_map(shards, mesh=mesh, in_specs=in_specs, out_specs=out_specs, check_vma=False)
```

```python
import functools

import jax
import jax.numpy as jnp
from jax import lax
from jax.experimental import pallas as pl
from jax.experimental.pallas import tpu as pltpu
from jax.sharding import PartitionSpec as P

HEADS = 16
LANES = 128
DEAD = -1e30


def normalize(rows):
    values = rows.astype(jnp.float32)
    centered = values - jnp.mean(values, axis=-1, keepdims=True)
    return centered * lax.rsqrt(jnp.mean(centered * centered, axis=-1, keepdims=True) + 1e-06)


def dot_t(a, b):
    return lax.dot_general(a, b, (((1,), (1,)), ((), ())), preferred_element_type=jnp.float32)


def attention_kernel(view_dev, tok, size, slots, obs_views, *refs):
    (cap_ref, q_ref, kb_ref, vb_ref, ko_ref, vo_ref, ka_ref, va_ref, kx_ref, vx_ref, w_ref,
     out_ref, s0, s1, e0, e1, m0, m1, r0, r1, heads) = refs
    step = pl.program_id(0)
    halo = slots - 1
    blocks = slots + obs_views

    def key_block(view, j, key):
        before, own, after, obs = (
            (kb_ref, ko_ref, ka_ref, kx_ref) if key else (vb_ref, vo_ref, va_ref, vx_ref)
        )
        if j >= slots:
            return obs[pl.ds((j - slots) * tok, tok), :]
        place = view + j
        reach = halo // 2
        if place < reach:
            return before[pl.ds(place * tok, tok), :]
        if place < reach + view_dev:
            return own[pl.ds((place - reach) * tok, tok), :]
        return after[pl.ds((place - reach - view_dev) * tok, tok), :]

    lane = lax.broadcasted_iota(jnp.int32, (tok, LANES), 1)
    per_tile = LANES // size
    units = [(view, head) for view in range(view_dev) for head in range(per_tile)]
    score, expo, top, inv = (s0, s1), (e0, e1), (m0, m1), (r0, r1)
    total = [None] * len(units)
    mixed = [None] * view_dev
    tiles = tok // LANES
    for t in range(len(units) + 2):
        a, b, c = t, t - 1, t - 2
        if a < len(units):
            view, head = units[a]
            q_all = q_ref[pl.ds(view * tok, tok), :]
            mine = (lane >= head * size) & (lane < (head + 1) * size)
            q = jnp.where(mine, q_all.astype(jnp.float32) * size ** -0.5, 0.0).astype(jnp.bfloat16)
            high = None
        if 0 <= b < len(units):
            low = None
            m_b = top[b % 2][...]
        if 0 <= c < len(units):
            acc = None
            r_c = inv[c % 2][...]
        for j in range(blocks):
            if a < len(units):
                s = dot_t(q, key_block(view, j, True))
                s = jnp.minimum(s, cap_ref[view : view + 1, pl.ds(j * tok, tok)])
                score[a % 2][:, pl.ds(j * tok, tok)] = s
                for i in range(tiles):
                    part = s[:, i * LANES : (i + 1) * LANES]
                    high = part if high is None else jnp.maximum(high, part)
            if 0 <= b < len(units):
                for i in range(tiles):
                    cols = pl.ds(j * tok + i * LANES, LANES)
                    e = jnp.exp(score[b % 2][:, cols] - m_b)
                    expo[b % 2][:, cols] = e
                    low = e if low is None else low + e
            if 0 <= c < len(units):
                probs = jnp.concatenate(
                    [
                        (expo[c % 2][:, pl.ds(j * tok + i * LANES, LANES)] * r_c).astype(jnp.bfloat16)
                        for i in range(tiles)
                    ],
                    axis=1,
                )
                part = jnp.dot(
                    probs, key_block(units[c][0], j, False), preferred_element_type=jnp.float32
                )
                acc = part if acc is None else acc + part
        if a < len(units):
            top[a % 2][...] = jnp.broadcast_to(
                jnp.max(high, axis=1, keepdims=True), (tok, LANES)
            )
        if 0 <= b < len(units):
            inv[b % 2][...] = jnp.broadcast_to(
                1.0 / jnp.sum(low, axis=1, keepdims=True), (tok, LANES)
            )
        if 0 <= c < len(units):
            view_c, head_c = units[c]
            if head_c == 0:
                mixed[view_c] = acc
            else:
                mixed[view_c] = jnp.where(lane >= head_c * size, acc, mixed[view_c])
            if head_c == per_tile - 1:
                heads[pl.ds(view_c * tok, tok), pl.ds(pl.multiple_of(step * LANES, LANES), LANES)] = (
                    mixed[view_c].astype(jnp.bfloat16)
                )

    @pl.when(step == pl.num_programs(0) - 1)
    def _():
        for view in range(view_dev):
            rows = pl.ds(view * tok, tok)
            out_ref[rows, :] = jnp.dot(
                heads[rows, :], w_ref[...], preferred_element_type=jnp.float32
            ).astype(jnp.bfloat16)


def attention(cap, query, before, own, after, obs, w_out, view_dev, tok, size, slots, obs_views):
    rows, width = query.shape
    pairs = width // LANES
    keys = (slots + obs_views) * tok

    def halves(array):
        n = array.shape[0]
        return (
            pl.BlockSpec((n, LANES), lambda p: (0, p)),
            pl.BlockSpec((n, LANES), lambda p: (0, p + pairs)),
        )

    whole = lambda shape: pl.BlockSpec(shape, lambda p: (0, 0))
    return pl.pallas_call(
        functools.partial(attention_kernel, view_dev, tok, size, slots, obs_views),
        grid=(pairs,),
        in_specs=[
            whole(cap.shape),
            pl.BlockSpec((rows, LANES), lambda p: (0, p)),
            *halves(before),
            *halves(own),
            *halves(after),
            *halves(obs),
            whole(w_out.shape),
        ],
        out_specs=whole((rows, width)),
        out_shape=jax.ShapeDtypeStruct((rows, width), jnp.bfloat16),
        scratch_shapes=[
            pltpu.VMEM((tok, keys), jnp.float32),
            pltpu.VMEM((tok, keys), jnp.float32),
            pltpu.VMEM((tok, keys), jnp.float32),
            pltpu.VMEM((tok, keys), jnp.float32),
            pltpu.VMEM((tok, LANES), jnp.float32),
            pltpu.VMEM((tok, LANES), jnp.float32),
            pltpu.VMEM((tok, LANES), jnp.float32),
            pltpu.VMEM((tok, LANES), jnp.float32),
            pltpu.VMEM((rows, width), jnp.bfloat16),
        ],
        compiler_params=pltpu.CompilerParams(vmem_limit_bytes=40 * 1024 * 1024),
    )(cap, query, before, before, own, own, after, after, obs, obs, w_out)


def gather_halving(rows, peers):
    bits = peers.bit_length() - 1
    turn = ([1] if bits > 1 else []) + list(range(bits - 1, 1, -1)) + ([0] if bits > 0 else [])
    part = rows.shape[0]
    held = rows[None]
    done = []
    for bit in turn:
        pairs = [(i, i ^ (1 << bit)) for i in range(peers)]
        came = lax.ppermute(held, "view", pairs)
        place = sum(1 for b in done if b < bit)
        low = 1 << place
        count = held.shape[0]
        shape = (count // low, 1, low, part, rows.shape[1])
        held = jnp.concatenate([held.reshape(shape), came.reshape(shape)], axis=1)
        held = held.reshape(2 * count, part, rows.shape[1])
        done.append(bit)
    return held.reshape(-1, rows.shape[1]), list(range(peers))


def shards(
    latents,
    mod_scale,
    observed,
    w_query,
    w_keyval,
    w_out,
    pair_views,
    pair_count,
    cond_views,
    cond_count,
    obs_count,
):
    view_dev, tok, width = latents.shape
    slots = pair_views.shape[1]
    reach = (slots - 1) // 2
    peers = lax.axis_size("view")
    views = view_dev * peers
    first = lax.axis_index("view") * view_dev
    obs_views = obs_count.shape[0]
    obs_norm = normalize(observed).astype(jnp.bfloat16)
    obs_rows, order = gather_halving(obs_norm, peers)
    modulated = (normalize(latents) * mod_scale[:, None, :]).astype(jnp.bfloat16)
    flat = modulated.reshape(view_dev * tok, width)
    up = [(i, (i + 1) % peers) for i in range(peers)]
    down = [(j, i) for i, j in up]
    edge = reach * tok
    before = lax.ppermute(flat[flat.shape[0] - edge :], "view", up)
    after = lax.ppermute(flat[:edge], "view", down)

    def project(rows, weight):
        return jnp.dot(rows, weight, preferred_element_type=jnp.float32).astype(jnp.bfloat16)

    query = project(flat, w_query)
    own_kv = project(flat, w_keyval)
    obs_kv = project(obs_rows, w_keyval)
    before_kv = project(before, w_keyval)
    after_kv = project(after, w_keyval)

    view_ids = first + jnp.arange(view_dev, dtype=jnp.int32)
    targets = (view_ids[:, None] + jnp.arange(slots, dtype=jnp.int32)[None, :] - reach) % views
    pair_live = jnp.arange(slots, dtype=jnp.int32)[None, :] < pair_count[:, None]
    window_live = jnp.any(
        (pair_views[:, None, :] == targets[:, :, None]) & pair_live[:, None, :], axis=-1
    )
    cond_live = jnp.arange(cond_views.shape[1], dtype=jnp.int32)[None, :] < cond_count[:, None]
    obs_ids = jnp.arange(obs_views, dtype=jnp.int32)
    obs_live = jnp.any(
        (cond_views[:, None, :] == obs_ids[None, :, None]) & cond_live[:, None, :], axis=-1
    )
    token_live = jnp.arange(tok, dtype=jnp.int32)[None, :] < obs_count[:, None]
    obs_key_live = (obs_live[:, :, None] & token_live[None, :, :]).reshape(
        view_dev, obs_views * tok
    )
    part = observed.shape[0]
    owner = lax.axis_index("view") ^ jnp.asarray(order, jnp.int32)
    obs_key_live = obs_key_live.reshape(view_dev, peers, part)[:, owner, :].reshape(
        view_dev, peers * part
    )
    live = jnp.concatenate([jnp.repeat(window_live, tok, axis=1), obs_key_live], axis=1)
    cap = jnp.where(live, jnp.finfo(jnp.float32).max, jnp.float32(DEAD))
    out = attention(
        cap, query, before_kv, own_kv, after_kv, obs_kv, w_out,
        view_dev, tok, width // HEADS, slots, obs_views,
    )
    return out.reshape(view_dev, tok, width)


def solution(mesh):
    in_specs = (
        P(("scene", "view"), None, None),
        P(("scene", "view"), None),
        P(("scene", "view"), None),
        P(),
        P(),
        P(),
        P(("scene", "view"), None),
        P(("scene", "view")),
        P(("scene", "view"), None),
        P(("scene", "view")),
        P("scene"),
    )
    out_specs = P(("scene", "view"), None, None)
    return jax.shard_map(shards, mesh=mesh, in_specs=in_specs, out_specs=out_specs, check_vma=False)
```

```python
import functools

import jax
import jax.numpy as jnp
from jax import lax
from jax.experimental import pallas as pl
from jax.experimental.pallas import tpu as pltpu
from jax.sharding import PartitionSpec as P

HEADS = 16
LANES = 128
DEAD = -1e30


def normalize(rows):
    values = rows.astype(jnp.float32)
    centered = values - jnp.mean(values, axis=-1, keepdims=True)
    return centered * lax.rsqrt(jnp.mean(centered * centered, axis=-1, keepdims=True) + 1e-06)


def dot_t(a, b):
    return lax.dot_general(a, b, (((1,), (1,)), ((), ())), preferred_element_type=jnp.float32)


def attention_kernel(view_dev, tok, size, slots, obs_views, *refs):
    (cap_ref, q_ref, k_ref, v_ref, w_ref,
     out_ref, s0, s1, e0, e1, m0, m1, r0, r1, heads) = refs
    step = pl.program_id(0)
    halo = slots - 1
    blocks = slots + obs_views

    def key_block(view, j, key):
        ref = k_ref if key else v_ref
        place = view + j if j < slots else view_dev + halo + j - slots
        return ref[pl.ds(place * tok, tok), :]

    lane = lax.broadcasted_iota(jnp.int32, (tok, LANES), 1)
    per_tile = LANES // size
    units = [(view, head) for view in range(view_dev) for head in range(per_tile)]
    score, expo, top, inv = (s0, s1), (e0, e1), (m0, m1), (r0, r1)
    total = [None] * len(units)
    mixed = [None] * view_dev
    tiles = tok // LANES
    for t in range(len(units) + 2):
        a, b, c = t, t - 1, t - 2
        if a < len(units):
            view, head = units[a]
            q_all = q_ref[pl.ds(view * tok, tok), :]
            mine = (lane >= head * size) & (lane < (head + 1) * size)
            q = jnp.where(mine, q_all.astype(jnp.float32) * size ** -0.5, 0.0).astype(jnp.bfloat16)
            high = None
        if 0 <= b < len(units):
            low = None
            m_b = top[b % 2][...]
        if 0 <= c < len(units):
            acc = None
            r_c = inv[c % 2][...]
        for j in range(blocks):
            if a < len(units):
                s = dot_t(q, key_block(view, j, True))
                s = jnp.minimum(s, cap_ref[view : view + 1, pl.ds(j * tok, tok)])
                score[a % 2][:, pl.ds(j * tok, tok)] = s
                for i in range(tiles):
                    part = s[:, i * LANES : (i + 1) * LANES]
                    high = part if high is None else jnp.maximum(high, part)
            if 0 <= b < len(units):
                for i in range(tiles):
                    cols = pl.ds(j * tok + i * LANES, LANES)
                    e = jnp.exp(score[b % 2][:, cols] - m_b)
                    expo[b % 2][:, cols] = e
                    low = e if low is None else low + e
            if 0 <= c < len(units):
                probs = jnp.concatenate(
                    [
                        (expo[c % 2][:, pl.ds(j * tok + i * LANES, LANES)] * r_c).astype(jnp.bfloat16)
                        for i in range(tiles)
                    ],
                    axis=1,
                )
                part = jnp.dot(
                    probs, key_block(units[c][0], j, False), preferred_element_type=jnp.float32
                )
                acc = part if acc is None else acc + part
        if a < len(units):
            top[a % 2][...] = jnp.broadcast_to(
                jnp.max(high, axis=1, keepdims=True), (tok, LANES)
            )
        if 0 <= b < len(units):
            inv[b % 2][...] = jnp.broadcast_to(
                1.0 / jnp.sum(low, axis=1, keepdims=True), (tok, LANES)
            )
        if 0 <= c < len(units):
            view_c, head_c = units[c]
            if head_c == 0:
                mixed[view_c] = acc
            else:
                mixed[view_c] = jnp.where(lane >= head_c * size, acc, mixed[view_c])
            if head_c == per_tile - 1:
                heads[pl.ds(view_c * tok, tok), pl.ds(pl.multiple_of(step * LANES, LANES), LANES)] = (
                    mixed[view_c].astype(jnp.bfloat16)
                )

    @pl.when(step == pl.num_programs(0) - 1)
    def _():
        for view in range(view_dev):
            rows = pl.ds(view * tok, tok)
            out_ref[rows, :] = jnp.dot(
                heads[rows, :], w_ref[...], preferred_element_type=jnp.float32
            ).astype(jnp.bfloat16)


def attention(cap, query, keyval, w_out, view_dev, tok, size, slots, obs_views):
    rows, width = query.shape
    pairs = width // LANES
    keys = (slots + obs_views) * tok

    whole = lambda shape: pl.BlockSpec(shape, lambda p: (0, 0))
    return pl.pallas_call(
        functools.partial(attention_kernel, view_dev, tok, size, slots, obs_views),
        grid=(pairs,),
        in_specs=[
            whole(cap.shape),
            pl.BlockSpec((rows, LANES), lambda p: (0, p)),
            pl.BlockSpec((keyval.shape[0], LANES), lambda p: (0, p)),
            pl.BlockSpec((keyval.shape[0], LANES), lambda p: (0, p + pairs)),
            whole(w_out.shape),
        ],
        out_specs=whole((rows, width)),
        out_shape=jax.ShapeDtypeStruct((rows, width), jnp.bfloat16),
        scratch_shapes=[
            pltpu.VMEM((tok, keys), jnp.float32),
            pltpu.VMEM((tok, keys), jnp.float32),
            pltpu.VMEM((tok, keys), jnp.float32),
            pltpu.VMEM((tok, keys), jnp.float32),
            pltpu.VMEM((tok, LANES), jnp.float32),
            pltpu.VMEM((tok, LANES), jnp.float32),
            pltpu.VMEM((tok, LANES), jnp.float32),
            pltpu.VMEM((tok, LANES), jnp.float32),
            pltpu.VMEM((rows, width), jnp.bfloat16),
        ],
        compiler_params=pltpu.CompilerParams(vmem_limit_bytes=40 * 1024 * 1024),
    )(cap, query, keyval, keyval, w_out)


def turns(peers):
    bits = peers.bit_length() - 1
    return ([1] if bits > 1 else []) + list(range(bits - 1, 1, -1)) + ([0] if bits > 0 else [])


def owners(peers):
    turn = turns(peers)
    return [sum(((p >> i) & 1) << bit for i, bit in enumerate(turn)) for p in range(peers)]


def project_kernel(peers, view_dev, tok):
    def kernel(lat_ref, mod_ref, obs_ref, wq_hbm, wkv_hbm, q_out, kv_out,
               wq, wkv, before, after, mod_b, mod_a, obs_all, rows_x, q_s, kv_s,
               w_sem, halo_send, halo_recv, mod_send, mod_recv, obs_send, obs_recv, out_sem):
        me = lax.axis_index("view")
        left = lax.rem(me + peers - 1, peers)
        right = lax.rem(me + 1, peers)
        turn = turns(peers)
        partners = [me + (1 << b) - (2 << b) * lax.rem(me // (1 << b), 2) for b in turn]
        edge, width = before.shape
        wide = kv_s.shape[1]

        loads = [
            pltpu.make_async_copy(wkv_hbm, wkv, w_sem.at[0]),
            pltpu.make_async_copy(wq_hbm, wq, w_sem.at[1]),
        ]
        for load in loads:
            load.start()
        obs_all[0] = obs_ref[...]
        barrier = pltpu.get_barrier_semaphore()
        for device in [left, right] + partners:
            pl.semaphore_signal(
                barrier, inc=1, device_id={"view": device}, device_id_type=pl.DeviceIdType.MESH
            )
        pl.semaphore_wait(barrier, 2 + len(partners))

        def send(src, dst, out, into, device):
            copy = pltpu.make_async_remote_copy(
                src_ref=src, dst_ref=dst, send_sem=out, recv_sem=into,
                device_id={"view": device}, device_id_type=pl.DeviceIdType.MESH,
            )
            copy.start()
            return copy

        def exchange(i):
            n = 1 << i
            return send(
                obs_all.at[pl.ds(0, n)], obs_all.at[pl.ds(n, n)],
                obs_send.at[i], obs_recv.at[i], partners[i],
            )

        stages = [exchange(0)]
        mods = [
            send(mod_ref, mod_b, mod_send.at[0], mod_recv.at[0], right),
            send(mod_ref, mod_a, mod_send.at[1], mod_recv.at[1], left),
        ]
        halos = [
            send(lat_ref, before, halo_send.at[0], halo_recv.at[0], right),
            send(lat_ref, after, halo_send.at[1], halo_recv.at[1], left),
        ]

        def advance(upto):
            while len(stages) < min(upto, len(turn)):
                stages[-1].wait()
                stages.append(exchange(len(stages)))

        step = 128

        def prepare(ref, mod):
            @pl.loop(0, edge // step)
            def _(i):
                at = pl.ds(pl.multiple_of(i * step, step), step)
                x = normalize(ref[at, :])
                x = x * mod[pl.ds(i // (tok // step), 1), :]
                rows_x[at, :] = x.astype(jnp.bfloat16)

        def multiply(weight, into, row, count):
            cols = 512

            @pl.loop(0, weight.shape[1] // cols)
            def _(i):
                at = pl.ds(pl.multiple_of(i * cols, cols), cols)
                into[pl.ds(row, count), at] = jnp.dot(
                    rows_x[pl.ds(0, count), :], weight[:, at], preferred_element_type=jnp.float32
                ).astype(jnp.bfloat16)

        outs = []

        def emit(row, count):
            out = pltpu.make_async_copy(
                kv_s.at[pl.ds(row, count)], kv_out.at[pl.ds(row, count)], out_sem.at[len(outs)]
            )
            out.start()
            outs.append(out)

        own = view_dev * tok
        prepare(lat_ref, mod_ref)
        for load in loads:
            load.wait()
        advance(2)
        multiply(wkv, kv_s, edge, own)
        emit(edge, own)
        advance(3)
        multiply(wq, q_s, 0, own)
        out_q = pltpu.make_async_copy(q_s, q_out, out_sem.at[5])
        out_q.start()
        advance(len(turn) - 1)

        part = obs_ref.shape[0]
        half = peers // 2
        base = own + 2 * edge
        group = max(1, step // part)

        def observed_half(which):
            @pl.loop(0, half // group)
            def _(i):
                x = obs_all[pl.ds(which * half + i * group, group)].astype(jnp.float32)
                x = x.reshape(group * part, width)
                rows_x[pl.ds(pl.multiple_of(i * group * part, group * part), group * part), :] = (
                    normalize(x).astype(jnp.bfloat16)
                )

            multiply(wkv, kv_s, base + which * half * part, half * part)
            emit(base + which * half * part, half * part)

        def halo(i, ref, mod, row):
            mods[i].wait()
            halos[i].wait()
            prepare(ref, mod)
            multiply(wkv, kv_s, row, edge)
            emit(row, edge)

        advance(len(turn))
        observed_half(0)
        halo(0, before, mod_b, 0)
        halo(1, after, mod_a, edge + own)
        stages[-1].wait()
        observed_half(1)
        for out in outs:
            out.wait()
        out_q.wait()

    return kernel


def project_all(latents, mod_scale, observed, w_query, w_keyval, peers, reach, tok):
    rows, width = latents.shape
    view_dev = rows // tok
    edge = reach * tok
    part = observed.shape[0]
    total = rows + 2 * edge + peers * part
    bits = peers.bit_length() - 1
    vmem = pl.BlockSpec(memory_space=pltpu.VMEM)
    hbm = pl.BlockSpec(memory_space=pl.ANY)
    bf16 = jnp.bfloat16
    return pl.pallas_call(
        project_kernel(peers, view_dev, tok),
        in_specs=[vmem, vmem, vmem, hbm, hbm],
        out_specs=[hbm, hbm],
        out_shape=[
            jax.ShapeDtypeStruct((rows, width), bf16),
            jax.ShapeDtypeStruct((total, 2 * width), bf16),
        ],
        scratch_shapes=[
            pltpu.VMEM(w_query.shape, bf16),
            pltpu.VMEM(w_keyval.shape, bf16),
            pltpu.VMEM((edge, width), bf16),
            pltpu.VMEM((edge, width), bf16),
            pltpu.VMEM(mod_scale.shape, jnp.float32),
            pltpu.VMEM(mod_scale.shape, jnp.float32),
            pltpu.VMEM((peers, part, width), bf16),
            pltpu.VMEM((max(rows, edge, peers * part // 2), width), bf16),
            pltpu.VMEM((rows, width), bf16),
            pltpu.VMEM((total, 2 * width), bf16),
            pltpu.SemaphoreType.DMA((2,)),
            pltpu.SemaphoreType.DMA((2,)),
            pltpu.SemaphoreType.DMA((2,)),
            pltpu.SemaphoreType.DMA((2,)),
            pltpu.SemaphoreType.DMA((2,)),
            pltpu.SemaphoreType.DMA((bits,)),
            pltpu.SemaphoreType.DMA((bits,)),
            pltpu.SemaphoreType.DMA((6,)),
        ],
        compiler_params=pltpu.CompilerParams(
            collective_id=0, has_side_effects=True, vmem_limit_bytes=48 * 1024 * 1024
        ),
    )(latents, mod_scale, observed, w_query, w_keyval)


def shards(
    latents,
    mod_scale,
    observed,
    w_query,
    w_keyval,
    w_out,
    pair_views,
    pair_count,
    cond_views,
    cond_count,
    obs_count,
):
    view_dev, tok, width = latents.shape
    slots = pair_views.shape[1]
    reach = (slots - 1) // 2
    peers = lax.axis_size("view")
    views = view_dev * peers
    first = lax.axis_index("view") * view_dev
    obs_views = obs_count.shape[0]
    query, keyval = project_all(
        latents.reshape(view_dev * tok, width), mod_scale, observed, w_query, w_keyval,
        peers, reach, tok,
    )
    view_ids = first + jnp.arange(view_dev, dtype=jnp.int32)
    targets = (view_ids[:, None] + jnp.arange(slots, dtype=jnp.int32)[None, :] - reach) % views
    pair_live = jnp.arange(slots, dtype=jnp.int32)[None, :] < pair_count[:, None]
    window_live = jnp.any(
        (pair_views[:, None, :] == targets[:, :, None]) & pair_live[:, None, :], axis=-1
    )
    cond_live = jnp.arange(cond_views.shape[1], dtype=jnp.int32)[None, :] < cond_count[:, None]
    obs_ids = jnp.arange(obs_views, dtype=jnp.int32)
    obs_live = jnp.any(
        (cond_views[:, None, :] == obs_ids[None, :, None]) & cond_live[:, None, :], axis=-1
    )
    token_live = jnp.arange(tok, dtype=jnp.int32)[None, :] < obs_count[:, None]
    obs_key_live = (obs_live[:, :, None] & token_live[None, :, :]).reshape(
        view_dev, obs_views * tok
    )
    part = observed.shape[0]
    owner = lax.axis_index("view") ^ jnp.asarray(owners(peers), jnp.int32)
    obs_key_live = obs_key_live.reshape(view_dev, peers, part)[:, owner, :].reshape(
        view_dev, peers * part
    )
    live = jnp.concatenate([jnp.repeat(window_live, tok, axis=1), obs_key_live], axis=1)
    cap = jnp.where(live, jnp.finfo(jnp.float32).max, jnp.float32(DEAD))
    out = attention(
        cap, query, keyval, w_out, view_dev, tok, width // HEADS, slots, obs_views,
    )
    return out.reshape(view_dev, tok, width)


def solution(mesh):
    in_specs = (
        P(("scene", "view"), None, None),
        P(("scene", "view"), None),
        P(("scene", "view"), None),
        P(),
        P(),
        P(),
        P(("scene", "view"), None),
        P(("scene", "view")),
        P(("scene", "view"), None),
        P(("scene", "view")),
        P("scene"),
    )
    out_specs = P(("scene", "view"), None, None)
    return jax.shard_map(shards, mesh=mesh, in_specs=in_specs, out_specs=out_specs, check_vma=False)
```

```python
import functools

import jax
import jax.numpy as jnp
from jax import lax
from jax.experimental import pallas as pl
from jax.experimental.pallas import tpu as pltpu
from jax.sharding import PartitionSpec as P

HEADS = 16
LANES = 128
DEAD = -1e30


def normalize(rows):
    values = rows.astype(jnp.float32)
    centered = values - jnp.mean(values, axis=-1, keepdims=True)
    return centered * lax.rsqrt(jnp.mean(centered * centered, axis=-1, keepdims=True) + 1e-06)


def dot_t(a, b):
    return lax.dot_general(a, b, (((1,), (1,)), ((), ())), preferred_element_type=jnp.float32)


def attention_kernel(peers, view_dev, tok, size, slots, obs_views, *refs):
    (pair_ref, pair_n, cond_ref, cond_n, obs_n, q_ref, k_ref, v_ref, w_ref,
     out_ref, cap_ref, s0, s1, e0, e1, m0, m1, r0, r1, heads) = refs
    step = pl.program_id(0)
    halo = slots - 1
    blocks = slots + obs_views

    @pl.when(step == 0)
    def _():
        me = lax.axis_index("view")
        views = view_dev * peers
        keys = obs_views * tok
        part = keys // peers
        column = lax.broadcasted_iota(jnp.int32, (1, keys), 1)
        slot = column // part
        owner = jnp.full((1, keys), me, jnp.int32)
        for i, bit in enumerate(turns(peers)):
            owner = owner ^ (((slot >> i) & 1) << bit)
        token = owner * part + column % part
        high = float(jnp.finfo(jnp.float32).max)
        for view in range(view_dev):
            for j in range(slots):
                target = lax.rem(me * view_dev + view + j - halo // 2 + views, views)
                live = jnp.bool_(False)
                for i in range(slots):
                    live = live | ((pair_ref[view, i] == target) & (i < pair_n[view]))
                cap_ref[view : view + 1, pl.ds(j * tok, tok)] = jnp.full(
                    (1, tok), jnp.where(live, high, DEAD), jnp.float32
                )
            seen = jnp.zeros((1, keys), jnp.bool_)
            for b in range(obs_views):
                live = jnp.bool_(False)
                for i in range(cond_ref.shape[1]):
                    live = live | ((cond_ref[view, i] == b) & (i < cond_n[view]))
                upto = b * tok + jnp.where(live, jnp.minimum(obs_n[b], tok), 0)
                seen = seen | ((token >= b * tok) & (token < upto))
            cap_ref[view : view + 1, pl.ds(slots * tok, keys)] = jnp.where(seen, high, DEAD)

    def key_block(view, j, key):
        ref = k_ref if key else v_ref
        place = view + j if j < slots else view_dev + halo + j - slots
        return ref[pl.ds(place * tok, tok), :]

    lane = lax.broadcasted_iota(jnp.int32, (tok, LANES), 1)
    per_tile = LANES // size
    units = [(view, head) for view in range(view_dev) for head in range(per_tile)]
    score, expo, top, inv = (s0, s1), (e0, e1), (m0, m1), (r0, r1)
    total = [None] * len(units)
    mixed = [None] * view_dev
    tiles = tok // LANES
    for t in range(len(units) + 2):
        a, b, c = t, t - 1, t - 2
        if a < len(units):
            view, head = units[a]
            q_all = q_ref[pl.ds(view * tok, tok), :]
            mine = (lane >= head * size) & (lane < (head + 1) * size)
            q = jnp.where(mine, q_all.astype(jnp.float32) * size ** -0.5, 0.0).astype(jnp.bfloat16)
            high = None
        if 0 <= b < len(units):
            low = None
            m_b = top[b % 2][...]
        if 0 <= c < len(units):
            acc = None
            r_c = inv[c % 2][...]
        for j in range(blocks):
            if a < len(units):
                s = dot_t(q, key_block(view, j, True))
                s = jnp.minimum(s, cap_ref[view : view + 1, pl.ds(j * tok, tok)])
                score[a % 2][:, pl.ds(j * tok, tok)] = s
                for i in range(tiles):
                    part = s[:, i * LANES : (i + 1) * LANES]
                    high = part if high is None else jnp.maximum(high, part)
            if 0 <= b < len(units):
                for i in range(tiles):
                    cols = pl.ds(j * tok + i * LANES, LANES)
                    e = jnp.exp(score[b % 2][:, cols] - m_b)
                    expo[b % 2][:, cols] = e
                    low = e if low is None else low + e
            if 0 <= c < len(units):
                probs = jnp.concatenate(
                    [
                        (expo[c % 2][:, pl.ds(j * tok + i * LANES, LANES)] * r_c).astype(jnp.bfloat16)
                        for i in range(tiles)
                    ],
                    axis=1,
                )
                part = jnp.dot(
                    probs, key_block(units[c][0], j, False), preferred_element_type=jnp.float32
                )
                acc = part if acc is None else acc + part
        if a < len(units):
            top[a % 2][...] = jnp.broadcast_to(
                jnp.max(high, axis=1, keepdims=True), (tok, LANES)
            )
        if 0 <= b < len(units):
            inv[b % 2][...] = jnp.broadcast_to(
                1.0 / jnp.sum(low, axis=1, keepdims=True), (tok, LANES)
            )
        if 0 <= c < len(units):
            view_c, head_c = units[c]
            if head_c == 0:
                mixed[view_c] = acc
            else:
                mixed[view_c] = jnp.where(lane >= head_c * size, acc, mixed[view_c])
            if head_c == per_tile - 1:
                heads[pl.ds(view_c * tok, tok), pl.ds(pl.multiple_of(step * LANES, LANES), LANES)] = (
                    mixed[view_c].astype(jnp.bfloat16)
                )

    @pl.when(step == pl.num_programs(0) - 1)
    def _():
        for view in range(view_dev):
            rows = pl.ds(view * tok, tok)
            out_ref[rows, :] = jnp.dot(
                heads[rows, :], w_ref[...], preferred_element_type=jnp.float32
            ).astype(jnp.bfloat16)


def attention(lists, query, keyval, w_out, peers, view_dev, tok, size, slots, obs_views):
    rows, width = query.shape
    pairs = width // LANES
    keys = (slots + obs_views) * tok

    whole = lambda shape: pl.BlockSpec(shape, lambda p: (0, 0))
    return pl.pallas_call(
        functools.partial(attention_kernel, peers, view_dev, tok, size, slots, obs_views),
        grid=(pairs,),
        in_specs=[
            *[pl.BlockSpec(memory_space=pltpu.SMEM)] * len(lists),
            pl.BlockSpec((rows, LANES), lambda p: (0, p)),
            pl.BlockSpec((keyval.shape[0], LANES), lambda p: (0, p)),
            pl.BlockSpec((keyval.shape[0], LANES), lambda p: (0, p + pairs)),
            whole(w_out.shape),
        ],
        out_specs=whole((rows, width)),
        out_shape=jax.ShapeDtypeStruct((rows, width), jnp.bfloat16),
        scratch_shapes=[
            pltpu.VMEM((view_dev, keys), jnp.float32),
            pltpu.VMEM((tok, keys), jnp.float32),
            pltpu.VMEM((tok, keys), jnp.float32),
            pltpu.VMEM((tok, keys), jnp.float32),
            pltpu.VMEM((tok, keys), jnp.float32),
            pltpu.VMEM((tok, LANES), jnp.float32),
            pltpu.VMEM((tok, LANES), jnp.float32),
            pltpu.VMEM((tok, LANES), jnp.float32),
            pltpu.VMEM((tok, LANES), jnp.float32),
            pltpu.VMEM((rows, width), jnp.bfloat16),
        ],
        compiler_params=pltpu.CompilerParams(vmem_limit_bytes=60 * 1024 * 1024),
    )(*lists, query, keyval, keyval, w_out)


def turns(peers):
    bits = peers.bit_length() - 1
    return (
        ([bits - 1] if bits > 2 else [])
        + ([1] if bits > 1 else [])
        + list(range(bits - 2, 1, -1))
        + ([0] if bits > 0 else [])
    )


def project_kernel(peers, view_dev, tok):
    def kernel(lat_ref, mod_ref, obs_ref, wq_hbm, wkv_hbm, q_out, kv_out,
               wq, wkv, before, after, mod_b, mod_a, obs_all, rows_x, q_s, kv_s,
               w_sem, halo_send, halo_recv, mod_send, mod_recv, obs_send, obs_recv, out_sem):
        me = lax.axis_index("view")
        left = lax.rem(me + peers - 1, peers)
        right = lax.rem(me + 1, peers)
        turn = turns(peers)
        partners = [me + (1 << b) - (2 << b) * lax.rem(me // (1 << b), 2) for b in turn]
        edge, width = before.shape
        wide = kv_s.shape[1]

        loads = [
            pltpu.make_async_copy(wkv_hbm, wkv, w_sem.at[0]),
            pltpu.make_async_copy(wq_hbm, wq, w_sem.at[1]),
        ]
        for load in loads:
            load.start()
        obs_all[0] = obs_ref[...]
        barrier = pltpu.get_barrier_semaphore()
        for device in [left, right] + partners:
            pl.semaphore_signal(
                barrier, inc=1, device_id={"view": device}, device_id_type=pl.DeviceIdType.MESH
            )
        pl.semaphore_wait(barrier, 2 + len(partners))

        def send(src, dst, out, into, device):
            copy = pltpu.make_async_remote_copy(
                src_ref=src, dst_ref=dst, send_sem=out, recv_sem=into,
                device_id={"view": device}, device_id_type=pl.DeviceIdType.MESH,
            )
            copy.start()
            return copy

        def exchange(i):
            n = 1 << i
            return send(
                obs_all.at[pl.ds(0, n)], obs_all.at[pl.ds(n, n)],
                obs_send.at[i], obs_recv.at[i], partners[i],
            )

        def halo_send_all(row, count, first):
            at = pl.ds(row, count)
            for i, (dst, device) in enumerate(((before, right), (after, left))):
                halos.append(
                    send(
                        lat_ref.at[at], dst.at[at],
                        halo_send.at[first + i], halo_recv.at[first + i], device,
                    )
                )

        halos = []
        stages = [exchange(0)]
        mods = [
            send(mod_ref, mod_b, mod_send.at[0], mod_recv.at[0], right),
            send(mod_ref, mod_a, mod_send.at[1], mod_recv.at[1], left),
        ]
        cut = edge // 2
        halo_send_all(0, cut, 0)

        def advance(upto):
            while len(stages) < min(upto, len(turn)):
                stages[-1].wait()
                stages.append(exchange(len(stages)))

        step = 128

        def prepare(ref, mod, row, count):
            @pl.loop(0, count // step)
            def _(i):
                at = pl.ds(pl.multiple_of(row + i * step, step), step)
                x = normalize(ref[at, :])
                x = x * mod[pl.ds(row // tok + i // (tok // step), 1), :]
                rows_x[pl.ds(pl.multiple_of(i * step, step), step), :] = x.astype(jnp.bfloat16)

        def multiply(weight, into, row, count):
            cols = 512

            @pl.loop(0, weight.shape[1] // cols)
            def _(i):
                at = pl.ds(pl.multiple_of(i * cols, cols), cols)
                into[pl.ds(row, count), at] = jnp.dot(
                    rows_x[pl.ds(0, count), :], weight[:, at], preferred_element_type=jnp.float32
                ).astype(jnp.bfloat16)

        outs = []

        def emit(row, count):
            out = pltpu.make_async_copy(
                kv_s.at[pl.ds(row, count)], kv_out.at[pl.ds(row, count)], out_sem.at[len(outs)]
            )
            out.start()
            outs.append(out)

        own = view_dev * tok
        prepare(lat_ref, mod_ref, 0, own)
        for load in loads:
            load.wait()
        advance(2)
        multiply(wkv, kv_s, edge, own)
        emit(edge, own)
        advance(3)
        halo_send_all(cut, edge - cut, 2)
        multiply(wq, q_s, 0, own)
        out_q = pltpu.make_async_copy(q_s, q_out, out_sem.at[7])
        out_q.start()
        advance(len(turn) - 1)

        part = obs_ref.shape[0]
        half = peers // 2
        base = own + 2 * edge
        group = max(1, step // part)

        def observed_half(which):
            @pl.loop(0, half // group)
            def _(i):
                x = obs_all[pl.ds(which * half + i * group, group)].astype(jnp.float32)
                x = x.reshape(group * part, width)
                rows_x[pl.ds(pl.multiple_of(i * group * part, group * part), group * part), :] = (
                    normalize(x).astype(jnp.bfloat16)
                )

            multiply(wkv, kv_s, base + which * half * part, half * part)
            emit(base + which * half * part, half * part)

        def halo(i, row, count):
            ref, mod, start = (before, mod_b, 0) if i % 2 == 0 else (after, mod_a, edge + own)
            halos[i].wait()
            prepare(ref, mod, row, count)
            multiply(wkv, kv_s, start + row, count)
            emit(start + row, count)

        mods[0].wait()
        mods[1].wait()
        halo(0, 0, cut)
        halo(1, 0, cut)
        advance(len(turn))
        observed_half(0)
        halo(2, cut, edge - cut)
        halo(3, cut, edge - cut)
        stages[-1].wait()
        observed_half(1)
        for out in outs:
            out.wait()
        out_q.wait()

    return kernel


def project_all(latents, mod_scale, observed, w_query, w_keyval, peers, reach, tok):
    rows, width = latents.shape
    view_dev = rows // tok
    edge = reach * tok
    part = observed.shape[0]
    total = rows + 2 * edge + peers * part
    bits = peers.bit_length() - 1
    vmem = pl.BlockSpec(memory_space=pltpu.VMEM)
    hbm = pl.BlockSpec(memory_space=pltpu.HBM)
    bf16 = jnp.bfloat16
    return pl.pallas_call(
        project_kernel(peers, view_dev, tok),
        in_specs=[vmem, vmem, vmem, hbm, hbm],
        out_specs=[hbm, hbm],
        out_shape=[
            jax.ShapeDtypeStruct((rows, width), bf16),
            jax.ShapeDtypeStruct((total, 2 * width), bf16),
        ],
        scratch_shapes=[
            pltpu.VMEM(w_query.shape, bf16),
            pltpu.VMEM(w_keyval.shape, bf16),
            pltpu.VMEM((edge, width), bf16),
            pltpu.VMEM((edge, width), bf16),
            pltpu.VMEM(mod_scale.shape, jnp.float32),
            pltpu.VMEM(mod_scale.shape, jnp.float32),
            pltpu.VMEM((peers, part, width), bf16),
            pltpu.VMEM((max(rows, edge, peers * part // 2), width), bf16),
            pltpu.VMEM((rows, width), bf16),
            pltpu.VMEM((total, 2 * width), bf16),
            pltpu.SemaphoreType.DMA((2,)),
            pltpu.SemaphoreType.DMA((4,)),
            pltpu.SemaphoreType.DMA((4,)),
            pltpu.SemaphoreType.DMA((2,)),
            pltpu.SemaphoreType.DMA((2,)),
            pltpu.SemaphoreType.DMA((bits,)),
            pltpu.SemaphoreType.DMA((bits,)),
            pltpu.SemaphoreType.DMA((8,)),
        ],
        compiler_params=pltpu.CompilerParams(
            collective_id=0, has_side_effects=True, vmem_limit_bytes=60 * 1024 * 1024
        ),
    )(latents, mod_scale, observed, w_query, w_keyval)


def shards(
    latents,
    mod_scale,
    observed,
    w_query,
    w_keyval,
    w_out,
    pair_views,
    pair_count,
    cond_views,
    cond_count,
    obs_count,
):
    view_dev, tok, width = latents.shape
    slots = pair_views.shape[1]
    reach = (slots - 1) // 2
    peers = lax.axis_size("view")
    obs_views = obs_count.shape[0]
    query, keyval = project_all(
        latents.reshape(view_dev * tok, width), mod_scale, observed, w_query, w_keyval,
        peers, reach, tok,
    )
    out = attention(
        (pair_views, pair_count, cond_views, cond_count, obs_count), query, keyval, w_out,
        peers, view_dev, tok, width // HEADS, slots, obs_views,
    )
    return out.reshape(view_dev, tok, width)


def solution(mesh):
    in_specs = (
        P(("scene", "view"), None, None),
        P(("scene", "view"), None),
        P(("scene", "view"), None),
        P(),
        P(),
        P(),
        P(("scene", "view"), None),
        P(("scene", "view")),
        P(("scene", "view"), None),
        P(("scene", "view")),
        P("scene"),
    )
    out_specs = P(("scene", "view"), None, None)
    return jax.shard_map(shards, mesh=mesh, in_specs=in_specs, out_specs=out_specs, check_vma=False)
```

```python
import functools

import jax
import jax.numpy as jnp
from jax import lax
from jax.experimental import pallas as pl
from jax.experimental.pallas import tpu as pltpu
from jax.sharding import PartitionSpec as P

HEADS = 16
LANES = 128
DEAD = -1e30


def normalize(rows):
    values = rows.astype(jnp.float32)
    centered = values - jnp.mean(values, axis=-1, keepdims=True)
    return centered * lax.rsqrt(jnp.mean(centered * centered, axis=-1, keepdims=True) + 1e-06)


def dot_t(a, b):
    return lax.dot_general(a, b, (((1,), (1,)), ((), ())), preferred_element_type=jnp.float32)


def attention_kernel(peers, view_dev, tok, size, slots, obs_views, *refs):
    (pair_ref, pair_n, cond_ref, cond_n, obs_n, q_ref, k_ref, v_ref, w_ref,
     out_ref, cap_ref, s0, s1, e0, e1, m0, m1, r0, r1, heads) = refs
    step = pl.program_id(0)
    halo = slots - 1
    blocks = slots + obs_views

    @pl.when(step == 0)
    def _():
        me = lax.axis_index("view")
        views = view_dev * peers
        keys = obs_views * tok
        part = keys // peers
        column = lax.broadcasted_iota(jnp.int32, (1, keys), 1)
        slot = column // part
        owner = jnp.full((1, keys), me, jnp.int32)
        for i, bit in enumerate(turns(peers)):
            owner = owner ^ (((slot >> i) & 1) << bit)
        token = owner * part + column % part
        high = float(jnp.finfo(jnp.float32).max)
        for view in range(view_dev):
            for j in range(slots):
                target = lax.rem(me * view_dev + view + j - halo // 2 + views, views)
                live = jnp.bool_(False)
                for i in range(slots):
                    live = live | ((pair_ref[view, i] == target) & (i < pair_n[view]))
                cap_ref[view : view + 1, pl.ds(j * tok, tok)] = jnp.full(
                    (1, tok), jnp.where(live, high, DEAD), jnp.float32
                )
            seen = jnp.zeros((1, keys), jnp.bool_)
            for b in range(obs_views):
                live = jnp.bool_(False)
                for i in range(cond_ref.shape[1]):
                    live = live | ((cond_ref[view, i] == b) & (i < cond_n[view]))
                upto = b * tok + jnp.where(live, jnp.minimum(obs_n[b], tok), 0)
                seen = seen | ((token >= b * tok) & (token < upto))
            cap_ref[view : view + 1, pl.ds(slots * tok, keys)] = jnp.where(seen, high, DEAD)

    def key_block(view, j, key):
        ref = k_ref if key else v_ref
        place = view + j if j < slots else view_dev + halo + j - slots
        return ref[pl.ds(place * tok, tok), :]

    lane = lax.broadcasted_iota(jnp.int32, (tok, LANES), 1)
    per_tile = LANES // size
    units = [(view, head) for view in range(view_dev) for head in range(per_tile)]
    score, expo, top, inv = (s0, s1), (e0, e1), (m0, m1), (r0, r1)
    total = [None] * len(units)
    mixed = [None] * view_dev
    tiles = tok // LANES
    for t in range(len(units) + 2):
        a, b, c = t, t - 1, t - 2
        if a < len(units):
            view, head = units[a]
            q_all = q_ref[pl.ds(view * tok, tok), :]
            mine = (lane >= head * size) & (lane < (head + 1) * size)
            q = jnp.where(mine, q_all.astype(jnp.float32) * size ** -0.5, 0.0).astype(jnp.bfloat16)
            high = None
        if 0 <= b < len(units):
            low = None
            m_b = top[b % 2][...]
        if 0 <= c < len(units):
            acc = None
            r_c = inv[c % 2][...]
        for j in range(blocks):
            if a < len(units):
                s = dot_t(q, key_block(view, j, True))
                s = jnp.minimum(s, cap_ref[view : view + 1, pl.ds(j * tok, tok)])
                score[a % 2][:, pl.ds(j * tok, tok)] = s
                for i in range(tiles):
                    part = s[:, i * LANES : (i + 1) * LANES]
                    high = part if high is None else jnp.maximum(high, part)
            if 0 <= b < len(units):
                for i in range(tiles):
                    cols = pl.ds(j * tok + i * LANES, LANES)
                    e = jnp.exp(score[b % 2][:, cols] - m_b)
                    expo[b % 2][:, cols] = e
                    low = e if low is None else low + e
            if 0 <= c < len(units):
                probs = jnp.concatenate(
                    [
                        (expo[c % 2][:, pl.ds(j * tok + i * LANES, LANES)] * r_c).astype(jnp.bfloat16)
                        for i in range(tiles)
                    ],
                    axis=1,
                )
                part = jnp.dot(
                    probs, key_block(units[c][0], j, False), preferred_element_type=jnp.float32
                )
                acc = part if acc is None else acc + part
        if a < len(units):
            top[a % 2][...] = jnp.broadcast_to(
                jnp.max(high, axis=1, keepdims=True), (tok, LANES)
            )
        if 0 <= b < len(units):
            inv[b % 2][...] = jnp.broadcast_to(
                1.0 / jnp.sum(low, axis=1, keepdims=True), (tok, LANES)
            )
        if 0 <= c < len(units):
            view_c, head_c = units[c]
            if head_c == 0:
                mixed[view_c] = acc
            else:
                mixed[view_c] = jnp.where(lane >= head_c * size, acc, mixed[view_c])
            if head_c == per_tile - 1:
                heads[pl.ds(view_c * tok, tok), pl.ds(pl.multiple_of(step * LANES, LANES), LANES)] = (
                    mixed[view_c].astype(jnp.bfloat16)
                )

    @pl.when(step == pl.num_programs(0) - 1)
    def _():
        for view in range(view_dev):
            rows = pl.ds(view * tok, tok)
            out_ref[rows, :] = jnp.dot(
                heads[rows, :], w_ref[...], preferred_element_type=jnp.float32
            ).astype(jnp.bfloat16)


def attention(lists, query, keyval, w_out, peers, view_dev, tok, size, slots, obs_views):
    rows, width = query.shape
    pairs = width // LANES
    keys = (slots + obs_views) * tok

    whole = lambda shape: pl.BlockSpec(shape, lambda p: (0, 0))
    return pl.pallas_call(
        functools.partial(attention_kernel, peers, view_dev, tok, size, slots, obs_views),
        grid=(pairs,),
        in_specs=[
            *[pl.BlockSpec(memory_space=pltpu.SMEM)] * len(lists),
            pl.BlockSpec((rows, LANES), lambda p: (0, p)),
            pl.BlockSpec((keyval.shape[0], LANES), lambda p: (0, p)),
            pl.BlockSpec((keyval.shape[0], LANES), lambda p: (0, p + pairs)),
            whole(w_out.shape),
        ],
        out_specs=whole((rows, width)),
        out_shape=jax.ShapeDtypeStruct((rows, width), jnp.bfloat16),
        scratch_shapes=[
            pltpu.VMEM((view_dev, keys), jnp.float32),
            pltpu.VMEM((tok, keys), jnp.float32),
            pltpu.VMEM((tok, keys), jnp.float32),
            pltpu.VMEM((tok, keys), jnp.float32),
            pltpu.VMEM((tok, keys), jnp.float32),
            pltpu.VMEM((tok, LANES), jnp.float32),
            pltpu.VMEM((tok, LANES), jnp.float32),
            pltpu.VMEM((tok, LANES), jnp.float32),
            pltpu.VMEM((tok, LANES), jnp.float32),
            pltpu.VMEM((rows, width), jnp.bfloat16),
        ],
        compiler_params=pltpu.CompilerParams(vmem_limit_bytes=60 * 1024 * 1024),
    )(*lists, query, keyval, keyval, w_out)


def turns(peers):
    bits = peers.bit_length() - 1
    return (
        ([bits - 1] if bits > 2 else [])
        + ([1] if bits > 1 else [])
        + list(range(bits - 2, 1, -1))
        + ([0] if bits > 0 else [])
    )


def project_kernel(peers, view_dev, tok):
    def kernel(lat_ref, mod_ref, obs_ref, wq_hbm, wkv_hbm, q_out, kv_out,
               wq, wkv, before, after, mod_b, mod_a, obs_all, rows_x, q_s, kv_s,
               w_sem, halo_send, halo_recv, mod_send, mod_recv, obs_send, obs_recv, out_sem):
        me = lax.axis_index("view")
        left = lax.rem(me + peers - 1, peers)
        right = lax.rem(me + 1, peers)
        turn = turns(peers)
        partners = [me + (1 << b) - (2 << b) * lax.rem(me // (1 << b), 2) for b in turn]
        edge, width = before.shape
        wide = kv_s.shape[1]

        loads = [
            pltpu.make_async_copy(wkv_hbm, wkv, w_sem.at[0]),
            pltpu.make_async_copy(wq_hbm, wq, w_sem.at[1]),
        ]
        for load in loads:
            load.start()
        obs_all[0] = obs_ref[...]
        barrier = pltpu.get_barrier_semaphore()
        for device in [left, right] + partners:
            pl.semaphore_signal(
                barrier, inc=1, device_id={"view": device}, device_id_type=pl.DeviceIdType.MESH
            )
        pl.semaphore_wait(barrier, 2 + len(partners))

        def send(src, dst, out, into, device):
            copy = pltpu.make_async_remote_copy(
                src_ref=src, dst_ref=dst, send_sem=out, recv_sem=into,
                device_id={"view": device}, device_id_type=pl.DeviceIdType.MESH,
            )
            copy.start()
            return copy

        def exchange(i):
            n = 1 << i
            return send(
                obs_all.at[pl.ds(0, n)], obs_all.at[pl.ds(n, n)],
                obs_send.at[i], obs_recv.at[i], partners[i],
            )

        def halo_send_all(row, count, first):
            at = pl.ds(row, count)
            for i, (dst, device) in enumerate(((before, right), (after, left))):
                halos.append(
                    send(
                        lat_ref.at[at], dst.at[at],
                        halo_send.at[first + i], halo_recv.at[first + i], device,
                    )
                )

        halos = []
        stages = [exchange(0)]
        mods = [
            send(mod_ref, mod_b, mod_send.at[0], mod_recv.at[0], right),
            send(mod_ref, mod_a, mod_send.at[1], mod_recv.at[1], left),
        ]
        cut = edge // 2
        quarter = cut // 2
        halo_send_all(0, quarter, 0)

        def advance(upto):
            while len(stages) < min(upto, len(turn)):
                stages[-1].wait()
                stages.append(exchange(len(stages)))

        step = 128

        def prepare(ref, mod, row, count):
            @pl.loop(0, count // step)
            def _(i):
                at = pl.ds(pl.multiple_of(row + i * step, step), step)
                x = normalize(ref[at, :])
                x = x * mod[pl.ds(row // tok + i // (tok // step), 1), :]
                rows_x[pl.ds(pl.multiple_of(i * step, step), step), :] = x.astype(jnp.bfloat16)

        def multiply(weight, into, row, count):
            cols = 512

            @pl.loop(0, weight.shape[1] // cols)
            def _(i):
                at = pl.ds(pl.multiple_of(i * cols, cols), cols)
                into[pl.ds(row, count), at] = jnp.dot(
                    rows_x[pl.ds(0, count), :], weight[:, at], preferred_element_type=jnp.float32
                ).astype(jnp.bfloat16)

        outs = []

        def emit(row, count):
            out = pltpu.make_async_copy(
                kv_s.at[pl.ds(row, count)], kv_out.at[pl.ds(row, count)], out_sem.at[len(outs)]
            )
            out.start()
            outs.append(out)

        own = view_dev * tok
        prepare(lat_ref, mod_ref, 0, own)
        for load in loads:
            load.wait()
        advance(2)
        multiply(wkv, kv_s, edge, own)
        emit(edge, own)
        advance(3)
        halo_send_all(quarter, cut - quarter, 2)
        halo_send_all(cut, edge - cut, 4)
        multiply(wq, q_s, 0, own)
        out_q = pltpu.make_async_copy(q_s, q_out, out_sem.at[7])
        out_q.start()
        advance(len(turn) - 1)

        part = obs_ref.shape[0]
        half = peers // 2
        base = own + 2 * edge
        group = max(1, step // part)

        def observed_half(which):
            @pl.loop(0, half // group)
            def _(i):
                x = obs_all[pl.ds(which * half + i * group, group)].astype(jnp.float32)
                x = x.reshape(group * part, width)
                rows_x[pl.ds(pl.multiple_of(i * group * part, group * part), group * part), :] = (
                    normalize(x).astype(jnp.bfloat16)
                )

            multiply(wkv, kv_s, base + which * half * part, half * part)
            emit(base + which * half * part, half * part)

        def halo(i, row, count):
            ref, mod, start = (before, mod_b, 0) if i % 2 == 0 else (after, mod_a, edge + own)
            for copy in (halos[i], halos[i + 2]) if row == 0 else (halos[i + 2],):
                copy.wait()
            prepare(ref, mod, row, count)
            multiply(wkv, kv_s, start + row, count)
            emit(start + row, count)

        mods[0].wait()
        mods[1].wait()
        halo(0, 0, cut)
        halo(1, 0, cut)
        advance(len(turn))
        observed_half(0)
        halo(2, cut, edge - cut)
        halo(3, cut, edge - cut)
        stages[-1].wait()
        observed_half(1)
        for out in outs:
            out.wait()
        out_q.wait()

    return kernel


def project_all(latents, mod_scale, observed, w_query, w_keyval, peers, reach, tok):
    rows, width = latents.shape
    view_dev = rows // tok
    edge = reach * tok
    part = observed.shape[0]
    total = rows + 2 * edge + peers * part
    bits = peers.bit_length() - 1
    vmem = pl.BlockSpec(memory_space=pltpu.VMEM)
    hbm = pl.BlockSpec(memory_space=pltpu.HBM)
    bf16 = jnp.bfloat16
    return pl.pallas_call(
        project_kernel(peers, view_dev, tok),
        in_specs=[vmem, vmem, vmem, hbm, hbm],
        out_specs=[hbm, hbm],
        out_shape=[
            jax.ShapeDtypeStruct((rows, width), bf16),
            jax.ShapeDtypeStruct((total, 2 * width), bf16),
        ],
        scratch_shapes=[
            pltpu.VMEM(w_query.shape, bf16),
            pltpu.VMEM(w_keyval.shape, bf16),
            pltpu.VMEM((edge, width), bf16),
            pltpu.VMEM((edge, width), bf16),
            pltpu.VMEM(mod_scale.shape, jnp.float32),
            pltpu.VMEM(mod_scale.shape, jnp.float32),
            pltpu.VMEM((peers, part, width), bf16),
            pltpu.VMEM((max(rows, edge, peers * part // 2), width), bf16),
            pltpu.VMEM((rows, width), bf16),
            pltpu.VMEM((total, 2 * width), bf16),
            pltpu.SemaphoreType.DMA((2,)),
            pltpu.SemaphoreType.DMA((6,)),
            pltpu.SemaphoreType.DMA((6,)),
            pltpu.SemaphoreType.DMA((2,)),
            pltpu.SemaphoreType.DMA((2,)),
            pltpu.SemaphoreType.DMA((bits,)),
            pltpu.SemaphoreType.DMA((bits,)),
            pltpu.SemaphoreType.DMA((8,)),
        ],
        compiler_params=pltpu.CompilerParams(
            collective_id=0, has_side_effects=True, vmem_limit_bytes=60 * 1024 * 1024
        ),
    )(latents, mod_scale, observed, w_query, w_keyval)


def shards(
    latents,
    mod_scale,
    observed,
    w_query,
    w_keyval,
    w_out,
    pair_views,
    pair_count,
    cond_views,
    cond_count,
    obs_count,
):
    view_dev, tok, width = latents.shape
    slots = pair_views.shape[1]
    reach = (slots - 1) // 2
    peers = lax.axis_size("view")
    obs_views = obs_count.shape[0]
    query, keyval = project_all(
        latents.reshape(view_dev * tok, width), mod_scale, observed, w_query, w_keyval,
        peers, reach, tok,
    )
    out = attention(
        (pair_views, pair_count, cond_views, cond_count, obs_count), query, keyval, w_out,
        peers, view_dev, tok, width // HEADS, slots, obs_views,
    )
    return out.reshape(view_dev, tok, width)


def solution(mesh):
    in_specs = (
        P(("scene", "view"), None, None),
        P(("scene", "view"), None),
        P(("scene", "view"), None),
        P(),
        P(),
        P(),
        P(("scene", "view"), None),
        P(("scene", "view")),
        P(("scene", "view"), None),
        P(("scene", "view")),
        P("scene"),
    )
    out_specs = P(("scene", "view"), None, None)
    return jax.shard_map(shards, mesh=mesh, in_specs=in_specs, out_specs=out_specs, check_vma=False)
```
